128 devices in a mesh: wide: 16 (over z, x), narrow: 8 (over y, core).
Axes of the slice: x: 4, y: 4, z: 4, core: 2. Of those that a mesh axis runs over, the one named last changes fastest.
Arguments:
- start_block: float32 [64, 6, 256, 512], P('narrow', None, 'wide'), may hold values from -6 to 6
- center_block: float32 [6, 6, 256, 512], P(None, None, 'wide'), may hold values from -0.1 to 13, as said below
- forward_blocks: float32 [4, 6, 6, 256, 512], P(None, None, None, 'wide'), may hold values from -0.1 to 0.1
- filter_cut: float32 [1], replicated, may hold values from 6 to 8
- filter_top: float32 [1], replicated, may hold values from 19 to 22
Outputs:
- basis: float32 [64, 6, 256, 512], P('narrow', None, 'wide')
- projected: float32 [64, 64], replicated
The draws below stay inside these ranges and needn't reach their ends.
Inputs may be any that keep to these rules, and one draw needn't show every extreme that they name: center_block[i, j] equals center_block[j, i] at every node; its diagonal entries lie in 6.5 to 13 and its other entries in -0.1 to 0.1.
All inputs are finite; a program needn't handle non-finite values.
Results may differ from the reference program's by a relative error of at most 0.0003.
Values sent between devices are 32-bit elements; how exact they have to be, the bound alone decides.
A program may use at most 128 MiB of HBM per device.

```python
import jax
import jax.numpy as jnp
from jax import lax

DOF = 6
M = 64
NR = 256
NC = 512
UNKNOWNS = 786432


field_count = 8


def char_region(key):
    subkeys = jax.random.split(key, 2)
    row_mid = jax.random.uniform(subkeys[0], (), jnp.float32, 0.25, 0.75)
    col_mid = jax.random.uniform(subkeys[1], (), jnp.float32, 0.0, 1.0)
    row_pos = jnp.arange(NR, dtype=jnp.float32)[:, None] / NR
    col_pos = jnp.arange(NC, dtype=jnp.float32)[None, :] / NC
    row_gap = row_pos - row_mid
    spread = (jnp.cos(2.0 * jnp.pi * (col_pos - col_mid)) - 1.0) / 0.3 - row_gap * row_gap / 0.05
    return jnp.exp(spread)


def draw_center_block(key, part):
    key = jax.random.fold_in(key, 11)
    diag_key, off_key, region_key = jax.random.split(key, 3)
    region = char_region(region_key)
    unit = jax.random.uniform(diag_key, (DOF, NR, NC), jnp.float32)
    rough = unit
    raw = jax.random.uniform(off_key, (DOF, DOF, NR, NC), jnp.float32, -0.1, 0.1)
    level = 0.6 * rough + 0.4 * (1.0 - region)[None]
    diagonal = 6.5 * jnp.exp(jnp.log(2.0) * level)
    identity = jnp.eye(DOF, dtype=jnp.float32)[:, :, None, None]
    symmetric = 0.5 * (raw + jnp.transpose(raw, (1, 0, 2, 3)))
    return symmetric * (1.0 - identity) + identity * diagonal[None]


def draw_start_block(key, part):
    key = jax.random.fold_in(key, 23)
    subkeys = jax.random.split(key, 5)
    row_pos = jnp.arange(NR, dtype=jnp.float32)[:, None] / NR
    col_pos = jnp.arange(NC, dtype=jnp.float32)[None, :] / NC
    row_freq = jax.random.uniform(subkeys[0], (field_count,), jnp.float32, 0.3, 2.0)
    col_freq = jax.random.randint(subkeys[1], (field_count,), 0, 4).astype(jnp.float32)
    phases = jax.random.uniform(subkeys[2], (field_count, DOF), jnp.float32, -jnp.pi, jnp.pi)
    weights = jax.random.uniform(subkeys[3], (M, field_count), jnp.float32, -0.85, 0.85)
    mixture = 0.5 * jax.random.normal(subkeys[4], (M, DOF, NR, NC), jnp.float32)
    for number in range(field_count):
        angles = 2.0 * jnp.pi * (row_freq[number] * row_pos + col_freq[number] * col_pos)
        pattern = jnp.cos(angles[None] + phases[number][:, None, None])
        mixture = mixture + weights[:, number][:, None, None, None] * pattern[None]
    return jnp.clip(mixture, -6.0, 6.0)


def shard_levels(key, dims, shards, low, top_value):
    factor_of = 1.0
    for axis_at, shards_of in shards:
        steps = jax.random.uniform(jax.random.fold_in(jax.random.fold_in(key, 6), axis_at), (shards_of,), jnp.float32, low / len(shards), top_value / len(shards))
        factor_of = factor_of * jnp.repeat(jnp.exp(steps), dims[axis_at] // shards_of).reshape((-1,) + (1,) * (len(dims) - 1 - axis_at))
    return factor_of


def setup_inputs(seed: int = 0) -> dict:
    key_of = jax.random.split(jax.random.key(seed), 6)
    start_block = draw_start_block(jax.random.fold_in(key_of[5], 71), 0)
    center_block = draw_center_block(jax.random.fold_in(key_of[5], 71), 0)
    forward_blocks = jnp.clip(jax.random.uniform(key_of[2], (4, DOF, DOF, NR, NC), jnp.float32, -0.1, 0.1) * shard_levels(key_of[2], (4, DOF, DOF, NR, NC), ((3, 16),), -0.4, 0.0), -0.1, 0.1)
    filter_cut = jnp.clip(jax.random.uniform(key_of[3], (1,), jnp.float32, 6.0, 8.0), 6.0, 8.0)
    filter_top = jnp.clip(jax.random.uniform(key_of[4], (1,), jnp.float32, 19.0, 22.0), 19.0, 22.0)
    return {"start_block": start_block, "center_block": center_block, "forward_blocks": forward_blocks, "filter_cut": filter_cut, "filter_top": filter_top}


OFFSETS = ((0, 1), (1, -1), (1, 0), (1, 1))
HIGHEST = lax.Precision.HIGHEST

def contract(coefficient, vectors):
    return jnp.sum(coefficient[None] * vectors[:, None], axis=2)

def contract_back(coefficient, vectors):
    return jnp.sum(coefficient[None] * vectors[:, :, None], axis=1)

def stiffness(vectors, center_block, forward_blocks):
    zero_row = jnp.zeros_like(vectors[:, :, :1])
    shifted_up = jnp.concatenate([vectors[:, :, 1:], zero_row], axis=2)
    summed = contract(center_block, vectors)
    for offset in range(4):
        step_row, step_col = OFFSETS[offset]
        source = shifted_up if step_row else vectors
        summed = summed + contract(forward_blocks[offset], jnp.roll(source, -step_col, axis=3))
        returned = contract_back(forward_blocks[offset], vectors)
        if step_row:
            returned = jnp.concatenate([zero_row, returned[:, :, :-1]], axis=2)
        summed = summed + jnp.roll(returned, step_col, axis=3)
    return summed

def inner_rows(left_side, right_side):
    return lax.dot_general(left_side, right_side, (((1,), (1,)), ((), ())), precision=HIGHEST)

def reference(start_block, center_block, forward_blocks, filter_cut, filter_top):
    middle = 0.5 * (filter_cut[0] + filter_top[0])
    half_width = 0.5 * (filter_top[0] - filter_cut[0])
    previous = start_block
    current = (stiffness(previous, center_block, forward_blocks) - middle * previous) / half_width
    for degree in range(2):
        following = 2.0 * (stiffness(current, center_block, forward_blocks) - middle * current) / half_width - previous
        previous, current = (current, following)
    flat = current.reshape(current.shape[0], -1)
    gram = inner_rows(flat, flat) / UNKNOWNS
    lower = jnp.linalg.cholesky(gram)
    basis_flat = lax.linalg.triangular_solve(lower, flat, left_side=True, lower=True)
    basis = basis_flat.reshape(current.shape)
    image = stiffness(basis, center_block, forward_blocks).reshape(current.shape[0], -1)
    projected = inner_rows(basis_flat, image) / UNKNOWNS
    return (basis, projected)
```

```python
import jax
import jax.numpy as jnp
from jax import lax
from jax.experimental import pallas as pl
from jax.experimental.pallas import tpu as pltpu
from jax.sharding import PartitionSpec as P

MESH = pl.DeviceIdType.MESH
HIGHEST = lax.Precision.HIGHEST
F32 = jnp.float32
BF16 = jnp.bfloat16
OFFSETS = ((0, 1), (1, -1), (1, 0), (1, 1))
NW, NN = 16, 8
ML, J, Q = 8, 6, 4
MB = 4
NB = ML // MB
PB = MB * J
PL = ML * J
VR_ = 32
FR_ = 24
VSZ = PL * Q * VR_
UNKNOWNS = 786432.0
SHIFTED = ((0, 1), (1, -1), (3, 1))


def lanes(rows=8):
    return lax.broadcasted_iota(jnp.int32, (rows, 128), 1)


def from_left(tiles):
    rolled = [pltpu.roll(t, 1, 1) for t in tiles]
    mask = lanes(tiles[0].shape[0]) == 0
    return [jnp.where(mask, rolled[(q - 1) % Q], rolled[q]) for q in range(Q)]


def from_right(tiles):
    rolled = [pltpu.roll(t, 127, 1) for t in tiles]
    mask = lanes(tiles[0].shape[0]) == 127
    return [jnp.where(mask, rolled[(q + 1) % Q], rolled[q]) for q in range(Q)]


def groups(count):
    return [(at, min(8, count - at)) for at in range(0, count, 8)]


def kernel(x, cen, fwd, cut, top, out, proj,
           vc, vl, vr, cv, fv, sh, cs, ch, hs, hr, eps, epr, mc, ml, mr, k5, wm, s, rb,
           a0, a1, ps, a2, pt, a3,
           ldsem, hss, hrs, css, crs, mss, mrs, ess, ers, a1s, a1r, a2s, a2r, a3s, a3r, bss, brs, locs):
    w, n = lax.axis_index("wide"), lax.axis_index("narrow")
    qme, gme = n // 2, n % 2

    vc6 = vc.reshape(2, ML, J, Q, VR_, 128)
    vc4 = vc.reshape(2 * PL, Q, VR_, 128)
    cv5 = cv.reshape(J, J, Q, 16, 128)
    fv6 = fv.reshape(4, J, J, Q, FR_, 128)
    mc4 = mc.reshape(NN, PL, 16, 128)
    rb5 = rb.reshape(NN, ML, J, 8, 128)

    xl, cl, fl = [], [], []
    for q in range(Q):
        col = pl.ds(128 * q, 128)
        xl.append(pltpu.make_async_copy(x.at[:, :, :, col], vc6.at[0, :, :, q, pl.ds(8, 16)], ldsem.at[q]))
        cl.append(pltpu.make_async_copy(cen.at[:, :, :, col], cv5.at[:, :, q], ldsem.at[4 + q]))
        fl.append(pltpu.make_async_copy(fwd.at[:, :, :, :, col], fv6.at[:, :, :, q, pl.ds(8, 16)], ldsem.at[8 + q]))
    for c in xl + fl + cl:
        c.start()

    barrier = pltpu.get_barrier_semaphore()
    for d in range(1, NN):
        pl.semaphore_signal(barrier, inc=1, device_id=(w, (n + d) % NN), device_id_type=MESH)
    for d in range(1, NW):
        pl.semaphore_signal(barrier, inc=1, device_id=((w + d) % NW, n), device_id_type=MESH)

    zero = jnp.zeros((8, 128), F32)

    def clear(p, _):
        for at in (8, 16):
            vc[pl.ds(pl.multiple_of(VSZ + p * VR_, 8) + at, 8), :] = zero
        return 0

    lax.fori_loop(0, PL * Q, clear, 0)

    @pl.when(w == 0)
    def _():
        for lv in range(3):
            for b in range(NB):
                hr[lv, b, 0] = jnp.zeros((Q * PB, 128), F32)
        ch[...] = jnp.zeros_like(ch)

    @pl.when(w == NW - 1)
    def _():
        for lv in range(4):
            for b in range(NB):
                hr[lv, b, 1] = jnp.zeros((Q * PB, 128), F32)

    up_dev, down_dev = (lax.rem(w + NW - 1, NW), n), (lax.rem(w + 1, NW), n)

    def halo(lv, b, side):
        return pltpu.make_async_remote_copy(
            src_ref=hs.at[lv, b, side], dst_ref=hr.at[lv, b, side], send_sem=hss.at[lv, b, side],
            recv_sem=hrs.at[lv, b, side], device_id=down_dev if side == 0 else up_dev, device_id_type=MESH)

    def extract(lv, b, buf, both):
        base = buf * VSZ + b * (PB * Q * VR_)
        for q in range(Q):
            for at, cnt in groups(PB):
                off = base + (at * Q + q) * VR_
                if both:
                    hs[lv, b, 0, pl.ds(q * PB + at, cnt), :] = vc[pl.ds(off + 23, cnt, stride=Q * VR_), :]
                hs[lv, b, 1, pl.ds(q * PB + at, cnt), :] = vc[pl.ds(off + 8, cnt, stride=Q * VR_), :]

    def send_halo(lv, b):
        @pl.when(w < NW - 1)
        def _():
            halo(lv, b, 0).start()

        @pl.when(w > 0)
        def _():
            halo(lv, b, 1).start()

    def shift_own(b, buf):
        def body(p, _):
            src = pl.multiple_of(buf * VSZ + (b * PB + p) * (Q * VR_), 8)
            dst = pl.multiple_of((b * PB + p) * (Q * VR_), 8)
            for g in range(2):
                tiles = [vc[pl.ds(src + q * VR_ + 8 + 8 * g, 8), :] for q in range(Q)]
                for q, t in enumerate(from_left(tiles)):
                    vl[pl.ds(dst + q * VR_ + 8 + 8 * g, 8), :] = t
                for q, t in enumerate(from_right(tiles)):
                    vr[pl.ds(dst + q * VR_ + 8 + 8 * g, 8), :] = t
            return 0

        lax.fori_loop(0, PB, body, 0)

    def unpack_halo(lv, b, buf):
        for side, row in ((0, 7), (1, 24)):
            for at, cnt in groups(PB):
                tiles = [hr[lv, b, side, pl.ds(q * PB + at, cnt), :] for q in range(Q)]
                base = (b * PB + at) * (Q * VR_)
                for ref, off, vals in ((vc, buf * VSZ, tiles), (vl, 0, from_left(tiles)), (vr, 0, from_right(tiles))):
                    for q in range(Q):
                        ref[pl.ds(off + base + q * VR_ + row, cnt, stride=Q * VR_), :] = vals[q]

    for c in xl:
        c.wait()
    for b in range(NB):
        extract(0, b, 0, True)
    pl.semaphore_wait(barrier, NN + NW - 2)
    for b in range(NB):
        send_halo(0, b)

    for c in fl:
        c.wait()
    for q in range(Q):
        for f in range(1, 4):
            for at, cnt in groups(36):
                cs[q, pl.ds((f - 1) * 36 + at, cnt), :] = fv[pl.ds(((f * 36 + at) * Q + q) * FR_ + 23, cnt, stride=Q * FR_), :]
    coef_halo = pltpu.make_async_remote_copy(
        src_ref=cs, dst_ref=ch, send_sem=css, recv_sem=crs, device_id=down_dev, device_id_type=MESH)

    @pl.when(w < NW - 1)
    def _():
        coef_halo.start()

    for b in range(NB):
        shift_own(b, 0)
    for at3, (f, step) in enumerate(SHIFTED):
        def body(p, _, at3=at3, f=f, step=step):
            src = pl.multiple_of((f * 36 + p) * (Q * FR_), 8)
            dst = pl.multiple_of((at3 * 36 + p) * (Q * FR_), 8)
            for g in range(2):
                tiles = [fv[pl.ds(src + q * FR_ + 8 + 8 * g, 8), :] for q in range(Q)]
                moved = from_left(tiles) if step == 1 else from_right(tiles)
                for q in range(Q):
                    sh[pl.ds(dst + q * FR_ + 8 + 8 * g, 8), :] = moved[q]
            return 0

        lax.fori_loop(0, 36, body, 0)

    @pl.when(w > 0)
    def _():
        coef_halo.wait_recv()

    for at, cnt in groups(36):
        for f, ref, slot, move in ((1, sh, 1, from_right), (2, fv, 2, None), (3, sh, 2, from_left)):
            tiles = [ch[q, pl.ds((f - 1) * 36 + at, cnt), :] for q in range(Q)]
            tiles = tiles if move is None else move(tiles)
            for q in range(Q):
                ref[pl.ds(((slot * 36 + at) * Q + q) * FR_ + 7, cnt, stride=Q * FR_), :] = tiles[q]
    for c in cl:
        c.wait()

    middle = 0.5 * (cut[0] + top[0])
    half_width = 0.5 * (top[0] - cut[0])

    stencil = [(cv, 16, 0, 0, False, 0, 0)]
    for f, (dr, dc) in enumerate(OFFSETS):
        stencil.append((fv, FR_, f * 36, 8, False, dc, dr))
    for ref, slot, (dr, dc) in ((sh, 0, (0, 1)), (sh, 1, (1, -1)), (fv, 2, (1, 0)), (sh, 2, (1, 1))):
        stencil.append((ref, FR_, slot * 36, 8 - dr, True, -dc, -dr))

    def apply(lv, b):
        cur = lax.rem(lv, 2) * VSZ
        nxt = VSZ - cur
        scale = jnp.where(lv == 0, 1.0, 2.0) / half_width
        vb = b * (PB * Q * VR_)

        def body(q, _):
            vq = q * VR_
            for g in range(2):
                acc = [[None] * J for _ in range(MB)]
                for ref, slot_rows, plane0, row0, transposed, dc, dr in stencil:
                    for j in range(J):
                        src = {0: vc, 1: vr, -1: vl}[dc]
                        base = pl.multiple_of(vb + vq + (cur if dc == 0 else 0), 8)
                        vs = [src[pl.ds(base + (m * J + j) * (Q * VR_) + 8 + 8 * g + dr, 8), :] for m in range(MB)]
                        for i in range(J):
                            plane = plane0 + (j * J + i if transposed else i * J + j)
                            cbase = pl.multiple_of(q * slot_rows, 8)
                            cf = ref[pl.ds(cbase + plane * (Q * slot_rows) + row0 + 8 * g, 8), :]
                            for m in range(MB):
                                term = cf * vs[m]
                                acc[m][i] = term if acc[m][i] is None else acc[m][i] + term
                for m in range(MB):
                    for i in range(J):
                        off = vb + vq
                        at = (m * J + i) * (Q * VR_) + 8 + 8 * g
                        here = vc[pl.ds(pl.multiple_of(off + cur, 8) + at, 8), :]
                        there = pl.ds(pl.multiple_of(off + nxt, 8) + at, 8)
                        vc[there, :] = (acc[m][i] - middle * here) * scale - vc[there, :]
            return 0

        lax.fori_loop(0, Q, body, 0)

    def main_copy(b, dst, sender):
        return pltpu.make_async_remote_copy(
            src_ref=vc4.at[pl.ds(PL + b * PB, PB), dst // 2, pl.ds(pl.multiple_of(8 + 8 * lax.rem(dst, 2), 8), 8)],
            dst_ref=mc4.at[sender, pl.ds(b * PB, PB), pl.ds(0, 8)],
            send_sem=mss.at[b, dst], recv_sem=mrs.at[b, sender], device_id=(w, dst), device_id_type=MESH)

    def own_main(b):
        return pltpu.make_async_copy(
            vc4.at[pl.ds(PL + b * PB, PB), qme, pl.ds(pl.multiple_of(8 + 8 * gme, 8), 8)],
            mc4.at[n, pl.ds(b * PB, PB), pl.ds(0, 8)], locs.at[b])

    def edge_copy(b, dst, sender):
        return pltpu.make_async_remote_copy(
            src_ref=eps.at[b, dst], dst_ref=epr.at[b, sender], send_sem=ess.at[b, dst], recv_sem=ers.at[b, sender],
            device_id=(w, dst), device_id_type=MESH)

    def own_edge(b):
        return pltpu.make_async_copy(eps.at[b, n], epr.at[b, n], locs.at[NB + b])

    def step(t, _):
        lv, b = t // NB, lax.rem(t, NB)
        buf = lax.rem(lv, 2)

        @pl.when(w > 0)
        def _():
            halo(lv, b, 0).wait_recv()

        @pl.when(w < NW - 1)
        def _():
            halo(lv, b, 1).wait_recv()

        unpack_halo(lv, b, buf)
        apply(lv, b)
        extract(lv + 1, b, 1 - buf, True)

        @pl.when(lv < 2)
        def _():
            send_halo(lv + 1, b)
            shift_own(b, 1 - buf)

        @pl.when(lv == 2)
        def _():
            @pl.when(w > 0)
            def _():
                halo(3, b, 1).start()

            for d in (4, 3, 5, 2, 6, 7, 1):
                dst = lax.rem(n + d, NN)
                main_copy(b, dst, n).start()
            own_main(b).start()

        return 0

    lax.fori_loop(0, 3 * NB, step, 0)

    lane = lanes()

    def edges(b, _):
        @pl.when(w < NW - 1)
        def _():
            halo(3, b, 1).wait_recv()

        def body(q, _):
            right, left = lax.rem(q + 1, Q), lax.rem(q + 3, Q)
            base = VSZ + b * (PB * Q * VR_)
            for g in range(2):
                dst = q * 2 + g
                pack = zero
                for p in range(PB):
                    at = p * (Q * VR_) + 8 + 8 * g
                    vright = vc[pl.ds(pl.multiple_of(base + right * VR_, 8) + at, 8), :]
                    vleft = vc[pl.ds(pl.multiple_of(base + left * VR_, 8) + at, 8), :]
                    pack = jnp.where(lane == p, vright if p == 0 else pltpu.roll(vright, p, 1), pack)
                    pack = jnp.where(lane == 32 + p, pltpu.roll(vleft, 33 + p, 1), pack)
                for k in range(PB // 8):
                    def row(at_q):
                        if g == 0:
                            off = pl.multiple_of(base + at_q * VR_, 8) + 8 * k * (Q * VR_) + 16
                            return vc[pl.ds(off, 8, stride=Q * VR_), :]
                        return hr[3, b, 1, pl.ds(pl.multiple_of(at_q * PB, 8) + 8 * k, 8), :]

                    eps[b, dst, pl.ds(8 * k, 8), :] = row(q)
                    pack = jnp.where(lane == 64 + k, pltpu.roll(row(right), 64 + k, 1), pack)
                    pack = jnp.where(lane == 72 + k, pltpu.roll(row(left), 73 + k, 1), pack)
                eps[b, dst, pl.ds(PB, 8), :] = pack
            return 0

        lax.fori_loop(0, Q, body, 0)
        for d in (4, 3, 5, 2, 6, 7, 1):
            edge_copy(b, lax.rem(n + d, NN), n).start()
        own_edge(b).start()
        return 0

    lax.fori_loop(0, NB, edges, 0)

    def own_coef(p, _):
        src = pl.multiple_of(p * (Q * 16) + qme * 16 + 8 * gme, 8)
        k5[pl.ds(pl.multiple_of(p * 8, 8), 8), :] = 0.5 * cv[pl.ds(src, 8), :]
        return 0

    def own_forward(p, _):
        src = pl.multiple_of(p * (Q * FR_) + qme * FR_ + 8 + 8 * gme, 8)
        k5[pl.ds(pl.multiple_of(288 + p * 8, 8), 8), :] = fv[pl.ds(src, 8), :]
        return 0

    lax.fori_loop(0, 36, own_coef, 0)
    lax.fori_loop(0, 144, own_forward, 0)

    def unpack(b, src):
        base = pl.multiple_of((src * PL + b * PB) * 16, 8)
        pack = epr[b, src, pl.ds(PB, 8), :]
        for p in range(PB):
            v = mc[pl.ds(base + p * 16, 8), :]
            mr[pl.ds(base + p * 16, 8), :] = jnp.where(lane == 127, pltpu.roll(pack, 127 - p, 1), pltpu.roll(v, 127, 1))
            ml[pl.ds(base + p * 16, 8), :] = jnp.where(lane == 0, pltpu.roll(pack, 96 - p, 1), pltpu.roll(v, 1, 1))
        for k in range(PB // 8):
            h = epr[b, src, pl.ds(8 * k, 8), :]
            there = pl.ds(base + 128 * k + 8, 8, stride=16)
            mc[there, :] = h
            mr[there, :] = jnp.where(lane == 127, pltpu.roll(pack, 63 - k, 1), pltpu.roll(h, 127, 1))
            ml[there, :] = jnp.where(lane == 0, pltpu.roll(pack, 56 - k, 1), pltpu.roll(h, 1, 1))

    half_stencil = ((mc, 0), (mr, 0), (ml, 1), (mc, 1), (mr, 1))

    def half_apply(b, src):
        base = pl.multiple_of((src * PL + b * PB) * 16, 8)
        wbase = pl.multiple_of((src * PL + b * PB) * 8, 8)
        acc = [[None] * J for _ in range(MB)]
        for f, (ref, dr) in enumerate(half_stencil):
            for j in range(J):
                vs = [ref[pl.ds(base + (m * J + j) * 16 + dr, 8), :] for m in range(MB)]
                for i in range(J):
                    cf = k5[pl.ds((f * 36 + i * J + j) * 8, 8), :]
                    for m in range(MB):
                        term = cf * vs[m]
                        acc[m][i] = term if acc[m][i] is None else acc[m][i] + term
        for m in range(MB):
            for i in range(J):
                wm[pl.ds(wbase + (m * J + i) * 8, 8), :] = acc[m][i]

    def meet(t, _):
        b, d = t // NN, lax.rem(t, NN)
        src = lax.rem(n + d, NN)

        @pl.when(d == 0)
        def _():
            own_main(b).wait()
            own_edge(b).wait()

        @pl.when(d > 0)
        def _():
            main_copy(b, n, src).wait_recv()
            edge_copy(b, n, src).wait_recv()

        unpack(b, src)
        half_apply(b, src)
        return 0

    lax.fori_loop(0, NB * NN, meet, 0)

    def split(v):
        hi = v.astype(BF16)
        return hi, (v - hi.astype(F32)).astype(BF16)

    for j in range(J):
        for r in range(8):
            col = pl.ds((j * 8 + r) * 128, 128)
            y = jnp.concatenate([mc[pl.ds((k * PL + j) * 16 + r, 8, stride=J * 16), :] for k in range(NN)], axis=0)
            z = jnp.concatenate([wm[pl.ds((k * PL + j) * 8 + r, 8, stride=J * 8), :] for k in range(NN)], axis=0)
            yhi, ylo = split(y)
            zhi, zlo = split(z)
            s[pl.ds(0, 64), col] = yhi
            s[pl.ds(64, 64), col] = zhi
            s[pl.ds(128, 64), col] = ylo
            s[pl.ds(192, 64), col] = zlo
    total = jnp.zeros((128, 256), F32)
    for k in range(12):
        col = pl.ds(k * 512, 512)
        left = jnp.concatenate([s[pl.ds(0, 64), col], s[pl.ds(128, 64), col]], axis=0)
        total = total + lax.dot_general(left, s[:, col], (((1,), (1,)), ((), ())), preferred_element_type=F32)
    a0[...] = ((total[0:64, 0:128] + (total[64:128, 0:128] + total[0:64, 128:256])) + total[64:128, 128:256]) / UNKNOWNS

    def piece1(dst, sender):
        return pltpu.make_async_remote_copy(
            src_ref=a0.at[pl.ds(pl.multiple_of(dst * 8, 8), 8)], dst_ref=a1.at[sender], send_sem=a1s.at[dst],
            recv_sem=a1r.at[sender], device_id=(w, dst), device_id_type=MESH)

    def piece2(dst, sender):
        return pltpu.make_async_remote_copy(
            src_ref=ps, dst_ref=a2.at[sender], send_sem=a2s.at[dst], recv_sem=a2r.at[sender],
            device_id=(dst, n), device_id_type=MESH)

    def piece3(dst, sender):
        return pltpu.make_async_remote_copy(
            src_ref=pt, dst_ref=a3.at[sender], send_sem=a3s.at[dst], recv_sem=a3r.at[sender],
            device_id=(w, dst), device_id_type=MESH)

    def exchange(piece, count, me):
        for d in range(1, count):
            piece(lax.rem(me + d, count), me).start()

    def collect(piece, count, me):
        for d in range(1, count):
            piece(me, lax.rem(me + d, count)).wait_recv()

    exchange(piece1, NN, n)
    a1[n] = a0[pl.ds(pl.multiple_of(n * 8, 8), 8), :]
    collect(piece1, NN, n)
    ps[...] = sum(a1[k] for k in range(1, NN)) + a1[0]
    exchange(piece2, NW, w)
    a2[w] = ps[...]
    collect(piece2, NW, w)
    pt[...] = sum(a2[k] for k in range(1, NW)) + a2[0]
    exchange(piece3, NN, n)
    a3[n] = pt[...]
    collect(piece3, NN, n)
    gz = jnp.concatenate([a3[k] for k in range(NN)], axis=0)

    lane64 = lanes(64)
    row64 = lax.broadcasted_iota(jnp.int32, (64, 128), 0)
    work = jnp.where(lane64 < 64, gz, (lane64 - 64 == row64).astype(F32))
    for k in range(64):
        pivot = work[k:k + 1, k:k + 1]
        factor = jnp.where(row64 > k, work[:, k:k + 1] / pivot, 0.0)
        work = work - factor * work[k:k + 1, :]
    diag = jnp.sum(jnp.where(lane64 == row64, work, 0.0), axis=1, keepdims=True)
    work = work * lax.rsqrt(diag)
    turned = pltpu.roll(work, 64, 1)
    twice = jnp.where(lane64 < 64, turned, work)
    mhi, mlo = split(twice)
    mix = jnp.concatenate([mhi, mlo], axis=0)

    def back(dst):
        return pltpu.make_async_remote_copy(
            src_ref=rb5.at[dst],
            dst_ref=out.at[:, :, pl.ds(pl.multiple_of(8 * gme, 8), 8), pl.ds(pl.multiple_of(128 * qme, 128), 128)],
            send_sem=bss.at[dst], recv_sem=brs.at[n], device_id=(w, dst), device_id_type=MESH)

    def back_arrival(sender):
        return pltpu.make_async_remote_copy(
            src_ref=rb5.at[sender],
            dst_ref=out.at[:, :, pl.ds(pl.multiple_of(8 * lax.rem(sender, 2), 8), 8),
                           pl.ds(pl.multiple_of(128 * (sender // 2), 128), 128)],
            send_sem=bss.at[sender], recv_sem=brs.at[sender], device_id=(w, sender), device_id_type=MESH)

    for tile in range(24):
        col = pl.ds(tile * 256, 256)
        right = jnp.concatenate([s[pl.ds(0, 64), col], s[pl.ds(128, 64), col]], axis=0)
        both = jnp.dot(mix, right, preferred_element_type=F32)
        basis = both[0:64] + both[64:128]
        for half in range(2):
            j, r = divmod(tile * 2 + half, 8)
            for k in range(NN):
                rb[pl.ds((k * PL + j) * 8 + r, 8, stride=J * 8), :] = basis[8 * k:8 * k + 8, 128 * half:128 * half + 128]
    for d in (4, 3, 5, 2, 6, 7, 1):
        back(lax.rem(n + d, NN)).start()
    own_back = pltpu.make_async_copy(
        rb5.at[n],
        out.at[:, :, pl.ds(pl.multiple_of(8 * gme, 8), 8), pl.ds(pl.multiple_of(128 * qme, 128), 128)],
        locs.at[2 * NB])
    own_back.start()

    minv = jnp.where(lane64 < 64, turned, 0.0)[:, 0:64]
    zmat = pltpu.roll(gz, 64, 1)[:, 0:64]
    half = jnp.dot(minv, zmat, precision=HIGHEST, preferred_element_type=F32) + lax.dot_general(
        minv, zmat, (((1,), (1,)), ((), ())), precision=HIGHEST, preferred_element_type=F32)
    proj[...] = lax.dot_general(half, minv, (((1,), (1,)), ((), ())), precision=HIGHEST, preferred_element_type=F32)

    for lv in range(3):
        for b in range(NB):
            @pl.when(w < NW - 1)
            def _():
                halo(lv, b, 0).wait_send()
    for lv in range(4):
        for b in range(NB):
            @pl.when(w > 0)
            def _():
                halo(lv, b, 1).wait_send()

    @pl.when(w < NW - 1)
    def _():
        coef_halo.wait_send()

    for d in range(1, NN):
        dst = lax.rem(n + d, NN)
        for b in range(NB):
            main_copy(b, dst, n).wait_send()
            edge_copy(b, dst, n).wait_send()
        piece1(dst, n).wait_send()
        piece3(dst, n).wait_send()
    for d in range(1, NW):
        piece2(lax.rem(w + d, NW), w).wait_send()
    own_back.wait()
    for d in range(1, NN):
        other = lax.rem(n + d, NN)
        back(other).wait_send()
        back_arrival(other).wait_recv()


def local(start_block, center_block, forward_blocks, filter_cut, filter_top):
    dma = pltpu.SemaphoreType.DMA
    vm = lambda *shape: pltpu.VMEM(shape, F32)
    anyspace = pl.BlockSpec(memory_space=pl.ANY)
    smem = pl.BlockSpec(memory_space=pltpu.SMEM)
    return pl.pallas_call(
        kernel,
        out_shape=(jax.ShapeDtypeStruct((ML, J, 16, 512), F32), jax.ShapeDtypeStruct((64, 64), F32)),
        in_specs=[anyspace, anyspace, anyspace, smem, smem],
        out_specs=(anyspace, pl.BlockSpec(memory_space=pltpu.VMEM)),
        scratch_shapes=[
            vm(2 * VSZ, 128), vm(VSZ, 128), vm(VSZ, 128),
            vm(36 * Q * 16, 128), vm(144 * Q * FR_, 128), vm(108 * Q * FR_, 128),
            vm(Q, 112, 128), vm(Q, 112, 128),
            vm(4, NB, 2, Q * PB, 128), vm(4, NB, 2, Q * PB, 128),
            vm(NB, NN, PB + 8, 128), vm(NB, NN, PB + 8, 128),
            vm(NN * PL * 16, 128), vm(NN * PL * 16, 128), vm(NN * PL * 16, 128),
            vm(180 * 8, 128), vm(NN * PL * 8, 128), pltpu.VMEM((256, 6144), BF16), vm(NN * PL * 8, 128),
            vm(64, 128), vm(NN, 8, 128), vm(8, 128), vm(NW, 8, 128), vm(8, 128), vm(NN, 8, 128),
            dma((12,)), dma((4, NB, 2)), dma((4, NB, 2)), dma(()), dma(()),
            dma((NB, NN)), dma((NB, NN)), dma((NB, NN)), dma((NB, NN)),
            dma((NN,)), dma((NN,)), dma((NW,)), dma((NW,)), dma((NN,)), dma((NN,)), dma((NN,)), dma((NN,)),
            dma((2 * NB + 1,)),
        ],
        compiler_params=pltpu.CompilerParams(
            collective_id=0, has_side_effects=True, vmem_limit_bytes=60 * 1024 * 1024),
    )(start_block, center_block, forward_blocks, filter_cut, filter_top)


def solution(mesh):
    in_specs = (
        P("narrow", None, "wide", None),
        P(None, None, "wide", None),
        P(None, None, None, "wide", None),
        P(),
        P(),
    )
    out_specs = (P("narrow", None, "wide", None), P())
    return jax.shard_map(local, mesh=mesh, in_specs=in_specs, out_specs=out_specs, check_vma=False)
```

```python
import jax
import jax.numpy as jnp
from jax import lax
from jax.experimental import pallas as pl
from jax.experimental.pallas import tpu as pltpu
from jax.sharding import PartitionSpec as P

MESH = pl.DeviceIdType.MESH
HIGHEST = lax.Precision.HIGHEST
F32 = jnp.float32
BF16 = jnp.bfloat16
OFFSETS = ((0, 1), (1, -1), (1, 0), (1, 1))
NW, NN = 16, 8
ML, J, Q = 8, 6, 4
MB = 4
NB = ML // MB
PB = MB * J
PL = ML * J
ER = (PB + 7) // 8 * 8
VR_ = 32
FR_ = 24
VSZ = PL * Q * VR_
UNKNOWNS = 786432.0
SHIFTED = ((0, 1), (1, -1), (3, 1))


def lanes(rows=8):
    return lax.broadcasted_iota(jnp.int32, (rows, 128), 1)


def from_left(tiles):
    rolled = [pltpu.roll(t, 1, 1) for t in tiles]
    mask = lanes(tiles[0].shape[0]) == 0
    return [jnp.where(mask, rolled[(q - 1) % Q], rolled[q]) for q in range(Q)]


def from_right(tiles):
    rolled = [pltpu.roll(t, 127, 1) for t in tiles]
    mask = lanes(tiles[0].shape[0]) == 127
    return [jnp.where(mask, rolled[(q + 1) % Q], rolled[q]) for q in range(Q)]


def groups(count):
    return [(at, min(8, count - at)) for at in range(0, count, 8)]


def kernel(x, cen, fwd, cut_hbm, top_hbm, out, proj,
           cut, top, vc, vl, vr, cv, fv, sh, cs, ch, hs, hr, eps, epr, mc, ml, mr, k5, wm, s, rb,
           a0, a1, ps, a2, pt, a3, pv, z0, z1, zp, z2,
           ldsem, hss, hrs, css, crs, mss, mrs, ess, ers, a1s, a1r, a2s, a2r, a3s, a3r, z1s, z1r, z2s, z2r, bss, brs, locs):
    w, n = lax.axis_index("wide"), lax.axis_index("narrow")
    qme, gme = n // 2, n % 2

    vc6 = vc.reshape(2, ML, J, Q, VR_, 128)
    vc4 = vc.reshape(2 * PL, Q, VR_, 128)
    cv5 = cv.reshape(J, J, Q, 16, 128)
    fv6 = fv.reshape(4, J, J, Q, FR_, 128)
    mc4 = mc.reshape(NN, PL, 16, 128)
    rb5 = rb.reshape(NN, ML, J, 8, 128)

    barrier = pltpu.get_barrier_semaphore()
    for d in range(1, NN):
        pl.semaphore_signal(barrier, inc=1, device_id=(w, (n + d) % NN), device_id_type=MESH)
    for d in range(1, NW):
        pl.semaphore_signal(barrier, inc=1, device_id=((w + d) % NW, n), device_id_type=MESH)

    xl, cl, fl = [], [], []
    for q in range(Q):
        col = pl.ds(128 * q, 128)
        xl.append(pltpu.make_async_copy(x.at[:, :, :, col], vc6.at[0, :, :, q, pl.ds(8, 16)], ldsem.at[q]))
        cl.append(pltpu.make_async_copy(cen.at[:, :, :, col], cv5.at[:, :, q], ldsem.at[4 + q]))
        fl.append(pltpu.make_async_copy(fwd.at[:, :, :, :, col], fv6.at[:, :, :, q, pl.ds(8, 16)], ldsem.at[8 + q]))
    scalars = [pltpu.make_async_copy(cut_hbm, cut, ldsem.at[12]), pltpu.make_async_copy(top_hbm, top, ldsem.at[13])]
    for c in fl + xl + cl + scalars:
        c.start()

    zero = jnp.zeros((8, 128), F32)

    def whole(v):
        return v if v.shape[0] == 8 else jnp.concatenate([v, zero[v.shape[0]:]], axis=0)

    def clear(p, _):
        for at in (8, 16):
            vc[pl.ds(pl.multiple_of(VSZ + p * VR_, 8) + at, 8), :] = zero
        return 0

    lax.fori_loop(0, PL * Q, clear, 0, unroll=8)

    @pl.when(w == 0)
    def _():
        for lv in range(3):
            for b in range(NB):
                hr[lv, b, 0] = jnp.zeros((Q * PB, 128), F32)
        ch[...] = jnp.zeros_like(ch)

    @pl.when(w == NW - 1)
    def _():
        for lv in range(4):
            for b in range(NB):
                hr[lv, b, 1] = jnp.zeros((Q * PB, 128), F32)

    up_dev, down_dev = (lax.rem(w + NW - 1, NW), n), (lax.rem(w + 1, NW), n)

    def halo(lv, b, side):
        return pltpu.make_async_remote_copy(
            src_ref=hs.at[lv, b, side], dst_ref=hr.at[lv, b, side], send_sem=hss.at[lv, b, side],
            recv_sem=hrs.at[lv, b, side], device_id=down_dev if side == 0 else up_dev, device_id_type=MESH)

    def extract(lv, b, buf, both):
        base = buf * VSZ + b * (PB * Q * VR_)
        for q in range(Q):
            for at, cnt in groups(PB):
                off = base + (at * Q + q) * VR_
                if both:
                    hs[lv, b, 0, pl.ds(q * PB + at, cnt), :] = vc[pl.ds(off + 23, cnt, stride=Q * VR_), :]
                hs[lv, b, 1, pl.ds(q * PB + at, cnt), :] = vc[pl.ds(off + 8, cnt, stride=Q * VR_), :]

    def send_halo(lv, b):
        @pl.when(w < NW - 1)
        def _():
            halo(lv, b, 0).start()

        @pl.when(w > 0)
        def _():
            halo(lv, b, 1).start()

    def shift_own(b, buf):
        def body(p, _):
            src = pl.multiple_of(buf * VSZ + (b * PB + p) * (Q * VR_), 8)
            dst = pl.multiple_of((b * PB + p) * (Q * VR_), 8)
            for g in range(2):
                tiles = [vc[pl.ds(src + q * VR_ + 8 + 8 * g, 8), :] for q in range(Q)]
                for q, t in enumerate(from_left(tiles)):
                    vl[pl.ds(dst + q * VR_ + 8 + 8 * g, 8), :] = t
                for q, t in enumerate(from_right(tiles)):
                    vr[pl.ds(dst + q * VR_ + 8 + 8 * g, 8), :] = t
            return 0

        lax.fori_loop(0, PB, body, 0, unroll=12)

    def unpack_halo(lv, b, buf):
        for side, row in ((0, 7), (1, 24)):
            for at, cnt in groups(PB):
                tiles = [hr[lv, b, side, pl.ds(q * PB + at, cnt), :] for q in range(Q)]
                base = (b * PB + at) * (Q * VR_)
                for ref, off, vals in ((vc, buf * VSZ, tiles), (vl, 0, from_left(tiles)), (vr, 0, from_right(tiles))):
                    for q in range(Q):
                        ref[pl.ds(off + base + q * VR_ + row, cnt, stride=Q * VR_), :] = vals[q]

    for c in fl:
        c.wait()
    for q in range(Q):
        for f in range(1, 4):
            for at, cnt in groups(36):
                cs[q, pl.ds((f - 1) * 36 + at, cnt), :] = fv[pl.ds(((f * 36 + at) * Q + q) * FR_ + 23, cnt, stride=Q * FR_), :]
    for at3, (f, step) in enumerate(SHIFTED):
        def body(p, _, at3=at3, f=f, step=step):
            src = pl.multiple_of((f * 36 + p) * (Q * FR_), 8)
            dst = pl.multiple_of((at3 * 36 + p) * (Q * FR_), 8)
            for g in range(2):
                tiles = [fv[pl.ds(src + q * FR_ + 8 + 8 * g, 8), :] for q in range(Q)]
                moved = from_left(tiles) if step == 1 else from_right(tiles)
                for q in range(Q):
                    sh[pl.ds(dst + q * FR_ + 8 + 8 * g, 8), :] = moved[q]
            return 0

        lax.fori_loop(0, 36, body, 0, unroll=12)

    for c in xl:
        c.wait()
    for b in range(NB):
        extract(0, b, 0, True)
    pl.semaphore_wait(barrier, NN + NW - 2)
    for b in range(NB):
        send_halo(0, b)

    coef_halo = pltpu.make_async_remote_copy(
        src_ref=cs, dst_ref=ch, send_sem=css, recv_sem=crs, device_id=down_dev, device_id_type=MESH)

    @pl.when(w < NW - 1)
    def _():
        coef_halo.start()

    for b in range(NB):
        shift_own(b, 0)

    @pl.when(w > 0)
    def _():
        coef_halo.wait_recv()

    for at, cnt in groups(36):
        for f, ref, slot, move in ((1, sh, 1, from_right), (2, fv, 2, None), (3, sh, 2, from_left)):
            tiles = [ch[q, pl.ds((f - 1) * 36 + at, cnt), :] for q in range(Q)]
            tiles = tiles if move is None else move(tiles)
            for q in range(Q):
                ref[pl.ds(((slot * 36 + at) * Q + q) * FR_ + 7, cnt, stride=Q * FR_), :] = tiles[q]
    for c in cl + scalars:
        c.wait()

    middle = 0.5 * (cut[0] + top[0])
    half_width = 0.5 * (top[0] - cut[0])

    stencil = [(cv, 16, 0, 0, False, 0, 0)]
    for f, (dr, dc) in enumerate(OFFSETS):
        stencil.append((fv, FR_, f * 36, 8, False, dc, dr))
    for ref, slot, (dr, dc) in ((sh, 0, (0, 1)), (sh, 1, (1, -1)), (fv, 2, (1, 0)), (sh, 2, (1, 1))):
        stencil.append((ref, FR_, slot * 36, 8 - dr, True, -dc, -dr))

    def main_copy(b, dst, sender):
        return pltpu.make_async_remote_copy(
            src_ref=vc4.at[pl.ds(PL + b * PB, PB), dst // 2, pl.ds(pl.multiple_of(8 + 8 * lax.rem(dst, 2), 8), 8)],
            dst_ref=mc4.at[sender, pl.ds(b * PB, PB), pl.ds(0, 8)],
            send_sem=mss.at[b, dst], recv_sem=mrs.at[b, sender], device_id=(w, dst), device_id_type=MESH)

    def own_main(b):
        return pltpu.make_async_copy(
            vc4.at[pl.ds(PL + b * PB, PB), qme, pl.ds(pl.multiple_of(8 + 8 * gme, 8), 8)],
            mc4.at[n, pl.ds(b * PB, PB), pl.ds(0, 8)], locs.at[b])

    def apply(lv, b):
        cur = lax.rem(lv, 2) * VSZ
        nxt = VSZ - cur
        scale = jnp.where(lv == 0, 1.0, 2.0) / half_width
        vb = b * (PB * Q * VR_)

        def body(k, _):
            q = lax.rem(qme + 1 + k, Q)
            vq = q * VR_
            for g in range(2):
                acc = [[None] * J for _ in range(MB)]
                for ref, slot_rows, plane0, row0, transposed, dc, dr in stencil:
                    for j in range(J):
                        src = {0: vc, 1: vr, -1: vl}[dc]
                        base = pl.multiple_of(vb + vq + (cur if dc == 0 else 0), 8)
                        vs = [src[pl.ds(base + (m * J + j) * (Q * VR_) + 8 + 8 * g + dr, 8), :] for m in range(MB)]
                        for i in range(J):
                            plane = plane0 + (j * J + i if transposed else i * J + j)
                            cbase = pl.multiple_of(q * slot_rows, 8)
                            cf = ref[pl.ds(cbase + plane * (Q * slot_rows) + row0 + 8 * g, 8), :]
                            for m in range(MB):
                                term = cf * vs[m]
                                acc[m][i] = term if acc[m][i] is None else acc[m][i] + term
                for m in range(MB):
                    for i in range(J):
                        off = vb + vq
                        at = (m * J + i) * (Q * VR_) + 8 + 8 * g
                        here = vc[pl.ds(pl.multiple_of(off + cur, 8) + at, 8), :]
                        there = pl.ds(pl.multiple_of(off + nxt, 8) + at, 8)
                        vc[there, :] = (acc[m][i] - middle * here) * scale - vc[there, :]

            @pl.when((lv == 2) & (k < Q - 1))
            def _():
                for g in range(2):
                    main_copy(b, 2 * q + g, n).start()

            return 0

        lax.fori_loop(0, Q, body, 0)

    def edge_copy(b, dst, sender):
        return pltpu.make_async_remote_copy(
            src_ref=eps.at[b, dst], dst_ref=epr.at[b, sender], send_sem=ess.at[b, dst], recv_sem=ers.at[b, sender],
            device_id=(w, dst), device_id_type=MESH)

    def own_edge(b):
        return pltpu.make_async_copy(eps.at[b, n], epr.at[b, n], locs.at[NB + b])

    lane = lanes()

    def edges(b):
        @pl.when(w < NW - 1)
        def _():
            halo(3, b, 1).wait_recv()

        def body(q, _):
            right, left = lax.rem(q + 1, Q), lax.rem(q + 3, Q)
            base = VSZ + b * (PB * Q * VR_)
            for g in range(2):
                dst = q * 2 + g
                pack = zero
                for p in range(PB):
                    at = p * (Q * VR_) + 8 + 8 * g
                    vright = vc[pl.ds(pl.multiple_of(base + right * VR_, 8) + at, 8), :]
                    vleft = vc[pl.ds(pl.multiple_of(base + left * VR_, 8) + at, 8), :]
                    pack = jnp.where(lane == 2 * p, vright if p == 0 else pltpu.roll(vright, 2 * p, 1), pack)
                    pack = jnp.where(lane == 2 * p + 1, pltpu.roll(vleft, 2 * p + 2, 1), pack)
                for k, (first, cnt) in enumerate(groups(PB)):
                    def row(at_q):
                        if g == 0:
                            off = pl.multiple_of(base + at_q * VR_, 8) + first * (Q * VR_) + 16
                            return vc[pl.ds(off, cnt, stride=Q * VR_), :]
                        return hr[3, b, 1, pl.ds(at_q * PB + first, cnt), :]

                    eps[b, dst, pl.ds(first, cnt), :] = row(q)
                    pack = jnp.where(lane == 64 + 2 * k, pltpu.roll(whole(row(right)), 64 + 2 * k, 1), pack)
                    pack = jnp.where(lane == 65 + 2 * k, pltpu.roll(whole(row(left)), 66 + 2 * k, 1), pack)
                eps[b, dst, pl.ds(ER, 8), :] = pack
            return 0

        lax.fori_loop(0, Q, body, 0)
        for d in (4, 3, 5, 2, 6, 7, 1):
            edge_copy(b, lax.rem(n + d, NN), n).start()
        own_edge(b).start()

    def step(t, _):
        late = jnp.minimum(t // 2, 1)
        lv = late * (1 + lax.rem(t, 2))
        b = (1 - late) * lax.rem(t, 2) + late * (t // 2 - 1)
        buf = lax.rem(lv, 2)


        @pl.when(w > 0)
        def _():
            halo(lv, b, 0).wait_recv()

        @pl.when(w < NW - 1)
        def _():
            halo(lv, b, 1).wait_recv()

        unpack_halo(lv, b, buf)
        apply(lv, b)
        extract(lv + 1, b, 1 - buf, True)

        @pl.when(lv < 2)
        def _():
            send_halo(lv + 1, b)
            shift_own(b, 1 - buf)

        @pl.when(lv == 2)
        def _():
            @pl.when(w > 0)
            def _():
                halo(3, b, 1).start()

            main_copy(b, 2 * qme + 1 - gme, n).start()
            own_main(b).start()

        return 0

    lax.fori_loop(0, 3 * NB, step, 0)

    def own_coef(p, _):
        src = pl.multiple_of(p * (Q * 16) + qme * 16 + 8 * gme, 8)
        k5[pl.ds(pl.multiple_of(p * 8, 8), 8), :] = 0.5 * cv[pl.ds(src, 8), :]
        return 0

    def own_forward(p, _):
        src = pl.multiple_of(p * (Q * FR_) + qme * FR_ + 8 + 8 * gme, 8)
        k5[pl.ds(pl.multiple_of(288 + p * 8, 8), 8), :] = fv[pl.ds(src, 8), :]
        return 0

    lax.fori_loop(0, 36, own_coef, 0, unroll=6)
    lax.fori_loop(0, 144, own_forward, 0, unroll=8)

    for b in range(NB):
        edges(b)
    for b in range(NB):
        for d in range(1, NN):
            main_copy(b, n, lax.rem(n + d, NN)).wait_recv()
        own_main(b).wait()

    def split(v):
        hi = v.astype(BF16)
        return hi, (v - hi.astype(F32)).astype(BF16)

    def fill(ref, slot, at):
        for j in range(J):
            for r in range(8):
                col = pl.ds((j * 8 + r) * 128, 128)
                v = jnp.concatenate(
                    [ref[pl.ds((k * PL + j) * slot + r, 8, stride=J * slot), :] for k in range(NN)], axis=0)
                hi, lo = split(v)
                s[pl.ds(at, 64), col] = hi
                s[pl.ds(at + 64, 64), col] = lo

    def products(at):
        total = jnp.zeros((128, 128), F32)
        for k in range(12):
            col = pl.ds(k * 512, 512)
            total = total + lax.dot_general(
                s[pl.ds(0, 128), col], s[pl.ds(at, 128), col], (((1,), (1,)), ((), ())), preferred_element_type=F32)
        both = total[0:64] + total[64:128]
        return (both + pltpu.roll(both, 64, 1)) / UNKNOWNS

    fill(mc, 16, 0)
    a0[...] = products(0)

    def piece1(dst, sender):
        return pltpu.make_async_remote_copy(
            src_ref=a0.at[pl.ds(pl.multiple_of(dst * 8, 8), 8)], dst_ref=a1.at[sender], send_sem=a1s.at[dst],
            recv_sem=a1r.at[sender], device_id=(w, dst), device_id_type=MESH)

    def piece2(dst, sender):
        return pltpu.make_async_remote_copy(
            src_ref=ps, dst_ref=a2.at[sender], send_sem=a2s.at[dst], recv_sem=a2r.at[sender],
            device_id=(dst, n), device_id_type=MESH)

    def piece3(dst, sender):
        return pltpu.make_async_remote_copy(
            src_ref=pt, dst_ref=a3.at[sender], send_sem=a3s.at[dst], recv_sem=a3r.at[sender],
            device_id=(w, dst), device_id_type=MESH)

    def whole1(dst, sender):
        return pltpu.make_async_remote_copy(
            src_ref=z0, dst_ref=z1.at[sender], send_sem=z1s.at[dst], recv_sem=z1r.at[sender],
            device_id=(w, dst), device_id_type=MESH)

    def whole2(dst, sender):
        return pltpu.make_async_remote_copy(
            src_ref=zp, dst_ref=z2.at[sender], send_sem=z2s.at[dst], recv_sem=z2r.at[sender],
            device_id=(dst, n), device_id_type=MESH)

    def exchange(piece, count, me):
        for d in range(1, count):
            piece(lax.rem(me + d, count), me).start()

    def collect(piece, count, me):
        for d in range(1, count):
            piece(me, lax.rem(me + d, count)).wait_recv()

    def added(ref, count):
        terms = [ref[k] for k in range(count)]
        while len(terms) > 1:
            terms = [terms[k] + terms[k + 1] for k in range(0, len(terms), 2)]
        return terms[0]

    def unpack(b, src):
        base = pl.multiple_of((src * PL + b * PB) * 16, 8)
        pack = epr[b, src, pl.ds(ER, 8), :]
        for p in range(PB):
            v = mc[pl.ds(base + p * 16, 8), :]
            sides = pltpu.roll(pack, 127 - 2 * p, 1)
            mr[pl.ds(base + p * 16, 8), :] = jnp.where(lane == 127, sides, pltpu.roll(v, 127, 1))
            ml[pl.ds(base + p * 16, 8), :] = jnp.where(lane == 0, sides, pltpu.roll(v, 1, 1))
        for k, (first, cnt) in enumerate(groups(PB)):
            h = epr[b, src, pl.ds(first, cnt), :]
            there = pl.ds(base + first * 16 + 8, cnt, stride=16)
            mc[there, :] = h
            mask = lanes(cnt)
            sides = pltpu.roll(pack, 63 - 2 * k, 1)[0:cnt]
            mr[there, :] = jnp.where(mask == 127, sides, pltpu.roll(h, 127, 1))
            ml[there, :] = jnp.where(mask == 0, sides, pltpu.roll(h, 1, 1))

    half_stencil = ((mc, 0), (mr, 0), (ml, 1), (mc, 1), (mr, 1))

    def half_apply(b, src):
        base = pl.multiple_of((src * PL + b * PB) * 16, 8)
        wbase = pl.multiple_of((src * PL + b * PB) * 8, 8)
        acc = [[None] * J for _ in range(MB)]
        for f, (ref, dr) in enumerate(half_stencil):
            for j in range(J):
                vs = [ref[pl.ds(base + (m * J + j) * 16 + dr, 8), :] for m in range(MB)]
                for i in range(J):
                    cf = k5[pl.ds((f * 36 + i * J + j) * 8, 8), :]
                    for m in range(MB):
                        term = cf * vs[m]
                        acc[m][i] = term if acc[m][i] is None else acc[m][i] + term
        for m in range(MB):
            for i in range(J):
                wm[pl.ds(wbase + (m * J + i) * 8, 8), :] = acc[m][i]

    def meet(t, _):
        b, d = t // NN, lax.rem(t, NN)
        src = lax.rem(n + d, NN)

        @pl.when(d == 0)
        def _():
            own_edge(b).wait()

        @pl.when(d > 0)
        def _():
            edge_copy(b, n, src).wait_recv()

        unpack(b, src)
        half_apply(b, src)
        return 0

    def meet_half(half):
        count = NB * NN // 2
        lax.fori_loop(half * count, (half + 1) * count, meet, 0)

    exchange(piece1, NN, n)
    a1[n] = a0[pl.ds(pl.multiple_of(n * 8, 8), 8), :]
    meet_half(0)
    collect(piece1, NN, n)
    ps[...] = added(a1, NN)
    exchange(piece2, NW, w)
    a2[w] = ps[...]
    meet_half(1)
    collect(piece2, NW, w)
    pt[...] = added(a2, NW)
    exchange(piece3, NN, n)
    a3[n] = pt[...]
    fill(wm, 8, 128)
    other = products(128)
    z0[...] = jnp.where(lanes(32) < 64, other[0:32], other[32:64])
    collect(piece3, NN, n)
    gram = jnp.concatenate([a3[k] for k in range(NN)], axis=0)
    exchange(whole1, NN, n)
    z1[n] = z0[...]

    lane64 = lanes(64)
    row64 = lax.broadcasted_iota(jnp.int32, (64, 128), 0)
    work = jnp.where(lane64 < 64, gram, (lane64 - 64 == row64).astype(F32))
    finished = []
    for k0 in range(0, 64, 4):
        first = 8 * len(finished)
        rows = row64[first:]
        column = [jnp.broadcast_to(work[:, k0 + t:k0 + t + 1], work.shape) for t in range(4)]
        line = [work[k0 + t - first:k0 + t - first + 1, :] for t in range(4)]
        for t in range(4):
            at = k0 + t - first
            factor = jnp.where(rows > k0 + t, column[t] * (1.0 / column[t][at:at + 1, :]), 0.0)
            for u in range(t + 1, 4):
                column[u] = column[u] - factor * column[u][at:at + 1, :]
                line[u] = line[u] - factor[at + u - t:at + u - t + 1, :] * line[t]
            work = work - factor * line[t]
        if k0 % 8 == 4:
            finished.append(work[0:8])
            work = work[8:]
    work = jnp.concatenate(finished, axis=0)
    diag = jnp.sum(jnp.where(lane64 == row64, work, 0.0), axis=1, keepdims=True)
    work = work * lax.rsqrt(diag)
    turned = pltpu.roll(work, 64, 1)
    twice = jnp.where(lane64 < 64, turned, work)
    mhi, mlo = split(twice)
    mix = jnp.concatenate([mhi, mlo], axis=0)

    collect(whole1, NN, n)
    zp[...] = added(z1, NN)
    exchange(whole2, NW, w)
    z2[w] = zp[...]

    def back(h, dst):
        return pltpu.make_async_remote_copy(
            src_ref=rb5.at[dst, :, pl.ds(3 * h, 3)],
            dst_ref=out.at[:, pl.ds(3 * h, 3), pl.ds(pl.multiple_of(8 * gme, 8), 8), pl.ds(pl.multiple_of(128 * qme, 128), 128)],
            send_sem=bss.at[h, dst], recv_sem=brs.at[h, n], device_id=(w, dst), device_id_type=MESH)

    def back_arrival(h, sender):
        return pltpu.make_async_remote_copy(
            src_ref=rb5.at[sender, :, pl.ds(3 * h, 3)],
            dst_ref=out.at[:, pl.ds(3 * h, 3), pl.ds(pl.multiple_of(8 * lax.rem(sender, 2), 8), 8),
                           pl.ds(pl.multiple_of(128 * (sender // 2), 128), 128)],
            send_sem=bss.at[h, sender], recv_sem=brs.at[h, sender], device_id=(w, sender), device_id_type=MESH)

    def own_back(h):
        return pltpu.make_async_copy(
            rb5.at[n, :, pl.ds(3 * h, 3)],
            out.at[:, pl.ds(3 * h, 3), pl.ds(pl.multiple_of(8 * gme, 8), 8), pl.ds(pl.multiple_of(128 * qme, 128), 128)],
            locs.at[2 * NB + h])

    for tile in range(24):
        col = pl.ds(tile * 256, 256)
        both = jnp.dot(mix, s[pl.ds(0, 128), col], preferred_element_type=F32)
        basis = both[0:64] + both[64:128]
        for half in range(2):
            j, r = divmod(tile * 2 + half, 8)
            for k in range(NN):
                rb[pl.ds((k * PL + j) * 8 + r, 8, stride=J * 8), :] = basis[8 * k:8 * k + 8, 128 * half:128 * half + 128]
        if tile % 12 == 11:
            for d in (4, 3, 5, 2, 6, 7, 1):
                back(tile // 12, lax.rem(n + d, NN)).start()
            own_back(tile // 12).start()


    collect(whole2, NW, w)
    other = added(z2, NW)
    other = jnp.concatenate([other, pltpu.roll(other, 64, 1)], axis=0)

    minv = jnp.where(lane64 < 64, turned, 0.0)[:, 0:64]
    zmat = other[:, 0:64]
    half = jnp.dot(minv, zmat, precision=HIGHEST, preferred_element_type=F32) + lax.dot_general(
        minv, zmat, (((1,), (1,)), ((), ())), precision=HIGHEST, preferred_element_type=F32)
    pv[...] = lax.dot_general(half, minv, (((1,), (1,)), ((), ())), precision=HIGHEST, preferred_element_type=F32)

    projected = pltpu.make_async_copy(pv, proj, locs.at[2 * NB + 2])
    projected.start()
    projected.wait()

    for lv in range(3):
        for b in range(NB):
            @pl.when(w < NW - 1)
            def _():
                halo(lv, b, 0).wait_send()
    for lv in range(4):
        for b in range(NB):
            @pl.when(w > 0)
            def _():
                halo(lv, b, 1).wait_send()

    @pl.when(w < NW - 1)
    def _():
        coef_halo.wait_send()

    for d in range(1, NN):
        dst = lax.rem(n + d, NN)
        for b in range(NB):
            main_copy(b, dst, n).wait_send()
            edge_copy(b, dst, n).wait_send()
        piece1(dst, n).wait_send()
        piece3(dst, n).wait_send()
        whole1(dst, n).wait_send()
    for d in range(1, NW):
        piece2(lax.rem(w + d, NW), w).wait_send()
        whole2(lax.rem(w + d, NW), w).wait_send()
    for h in range(2):
        own_back(h).wait()
        for d in range(1, NN):
            back(h, lax.rem(n + d, NN)).wait_send()
            back_arrival(h, lax.rem(n + d, NN)).wait_recv()


def hand_over(basis, projected, basis_out, projected_out):
    basis_out[...] = basis[...]
    projected_out[...] = projected[...]


def local(start_block, center_block, forward_blocks, filter_cut, filter_top):
    dma = pltpu.SemaphoreType.DMA
    vm = lambda *shape: pltpu.VMEM(shape, F32)
    anyspace = pl.BlockSpec(memory_space=pl.ANY)
    block = pl.BlockSpec((2, J, 16, 512), lambda k: (k, 0, 0, 0))
    small = pl.BlockSpec((64, 64), lambda k: (0, 0))
    basis, projected = pl.pallas_call(
        kernel,
        out_shape=(jax.ShapeDtypeStruct((ML, J, 16, 512), F32), jax.ShapeDtypeStruct((64, 64), F32)),
        in_specs=[anyspace] * 5,
        out_specs=(anyspace, anyspace),
        scratch_shapes=[
            pltpu.SMEM((1,), F32), pltpu.SMEM((1,), F32),
            vm(2 * VSZ, 128), vm(VSZ, 128), vm(VSZ, 128),
            vm(36 * Q * 16, 128), vm(144 * Q * FR_, 128), vm(108 * Q * FR_, 128),
            vm(Q, 112, 128), vm(Q, 112, 128),
            vm(4, NB, 2, Q * PB, 128), vm(4, NB, 2, Q * PB, 128),
            vm(NB, NN, ER + 8, 128), vm(NB, NN, ER + 8, 128),
            vm(NN * PL * 16, 128), vm(NN * PL * 16, 128), vm(NN * PL * 16, 128),
            vm(180 * 8, 128), vm(NN * PL * 8, 128), pltpu.VMEM((256, 6144), BF16), vm(NN * PL * 8, 128),
            vm(64, 128), vm(NN, 8, 128), vm(8, 128), vm(NW, 8, 128), vm(8, 128), vm(NN, 8, 128), vm(64, 64),
            vm(32, 128), vm(NN, 32, 128), vm(32, 128), vm(NW, 32, 128),
            dma((14,)), dma((4, NB, 2)), dma((4, NB, 2)), dma(()), dma(()),
            dma((NB, NN)), dma((NB, NN)), dma((NB, NN)), dma((NB, NN)),
            dma((NN,)), dma((NN,)), dma((NW,)), dma((NW,)), dma((NN,)), dma((NN,)),
            dma((NN,)), dma((NN,)), dma((NW,)), dma((NW,)), dma((2, NN)), dma((2, NN)),
            dma((2 * NB + 3,)),
        ],
        compiler_params=pltpu.CompilerParams(
            collective_id=0, has_side_effects=True, vmem_limit_bytes=60 * 1024 * 1024),
    )(start_block, center_block, forward_blocks, filter_cut, filter_top)
    return pl.pallas_call(
        hand_over,
        out_shape=(jax.ShapeDtypeStruct(basis.shape, F32), jax.ShapeDtypeStruct(projected.shape, F32)),
        grid=(4,),
        in_specs=[block, small],
        out_specs=(block, small),
    )(basis, projected)


def solution(mesh):
    in_specs = (
        P("narrow", None, "wide", None),
        P(None, None, "wide", None),
        P(None, None, None, "wide", None),
        P(),
        P(),
    )
    out_specs = (P("narrow", None, "wide", None), P())
    return jax.shard_map(local, mesh=mesh, in_specs=in_specs, out_specs=out_specs, check_vma=False)
```

```python
import jax
import jax.numpy as jnp
from jax import lax
from jax.experimental import pallas as pl
from jax.experimental.pallas import tpu as pltpu
from jax.sharding import PartitionSpec as P

MESH = pl.DeviceIdType.MESH
HIGHEST = lax.Precision.HIGHEST
F32 = jnp.float32
BF16 = jnp.bfloat16
OFFSETS = ((0, 1), (1, -1), (1, 0), (1, 1))
NW, NN = 16, 8
ML, J, Q = 8, 6, 4
MB = 4
NB = ML // MB
PB = MB * J
PL = ML * J
ER = (PB + 7) // 8 * 8
VR_ = 32
FR_ = 24
VSZ = PL * Q * VR_
UNKNOWNS = 786432.0
SHIFTED = ((0, 1), (1, -1), (3, 1))


def lanes(rows=8):
    return lax.broadcasted_iota(jnp.int32, (rows, 128), 1)


def from_left(tiles):
    rolled = [pltpu.roll(t, 1, 1) for t in tiles]
    mask = lanes(tiles[0].shape[0]) == 0
    return [jnp.where(mask, rolled[(q - 1) % Q], rolled[q]) for q in range(Q)]


def from_right(tiles):
    rolled = [pltpu.roll(t, 127, 1) for t in tiles]
    mask = lanes(tiles[0].shape[0]) == 127
    return [jnp.where(mask, rolled[(q + 1) % Q], rolled[q]) for q in range(Q)]


def groups(count):
    return [(at, min(8, count - at)) for at in range(0, count, 8)]


def kernel(x, cen, fwd, cut_hbm, top_hbm, out, proj,
           cut, top, vc, vl, vr, cv, fv, sh, cs, ch, hs, hr, eps, epr, mc, ml, mr, k5, wm, s, rb,
           a0, a1, ps, a2, pt, a3, pv, z0, z1, zp, z2,
           ldsem, hss, hrs, css, crs, mss, mrs, ess, ers, a1s, a1r, a2s, a2r, a3s, a3r, z1s, z1r, z2s, z2r, bss, brs, locs):
    w, n = lax.axis_index("wide"), lax.axis_index("narrow")
    qme, gme = n // 2, n % 2

    vc6 = vc.reshape(2, ML, J, Q, VR_, 128)
    vc4 = vc.reshape(2 * PL, Q, VR_, 128)
    cv5 = cv.reshape(J, J, Q, 16, 128)
    fv6 = fv.reshape(4, J, J, Q, FR_, 128)
    mc4 = mc.reshape(NN, PL, 16, 128)
    rb5 = rb.reshape(NN, ML, J, 8, 128)

    barrier = pltpu.get_barrier_semaphore()
    for d in range(1, NN):
        pl.semaphore_signal(barrier, inc=1, device_id=(w, (n + d) % NN), device_id_type=MESH)
    for d in range(1, NW):
        pl.semaphore_signal(barrier, inc=1, device_id=((w + d) % NW, n), device_id_type=MESH)

    xl, cl, fl = [], [], []
    for q in range(Q):
        col = pl.ds(128 * q, 128)
        xl.append(pltpu.make_async_copy(x.at[:, :, :, col], vc6.at[0, :, :, q, pl.ds(8, 16)], ldsem.at[q]))
        cl.append(pltpu.make_async_copy(cen.at[:, :, :, col], cv5.at[:, :, q], ldsem.at[4 + q]))
        fl.append(pltpu.make_async_copy(fwd.at[:, :, :, :, col], fv6.at[:, :, :, q, pl.ds(8, 16)], ldsem.at[8 + q]))
    scalars = [pltpu.make_async_copy(cut_hbm, cut, ldsem.at[12]), pltpu.make_async_copy(top_hbm, top, ldsem.at[13])]
    for c in xl + fl + cl + scalars:
        c.start()

    zero = jnp.zeros((8, 128), F32)

    def whole(v):
        return v if v.shape[0] == 8 else jnp.concatenate([v, zero[v.shape[0]:]], axis=0)

    def clear(p, _):
        for at in (8, 16):
            vc[pl.ds(pl.multiple_of(VSZ + p * VR_, 8) + at, 8), :] = zero
        return 0

    lax.fori_loop(0, PL * Q, clear, 0, unroll=8)

    def clear_rows(p, _):
        for ref in (vc, vl, vr):
            for at in (0, 24):
                ref[pl.ds(pl.multiple_of(p * VR_, 8) + at, 8), :] = zero
        return 0

    def clear_coef(p, _):
        for ref, slot in ((sh, 1), (sh, 2), (fv, 2)):
            ref[pl.ds(pl.multiple_of(slot * 36 * Q * FR_ + p * FR_, 8), 8), :] = zero
        return 0

    lax.fori_loop(0, PL * Q, clear_rows, 0, unroll=8)
    lax.fori_loop(0, 36 * Q, clear_coef, 0, unroll=8)

    @pl.when(w == 0)
    def _():
        for lv in range(3):
            for b in range(NB):
                hr[lv, b, 0] = jnp.zeros((Q * PB, 128), F32)
        ch[...] = jnp.zeros_like(ch)

    @pl.when(w == NW - 1)
    def _():
        for lv in range(4):
            for b in range(NB):
                hr[lv, b, 1] = jnp.zeros((Q * PB, 128), F32)

    up_dev, down_dev = (lax.rem(w + NW - 1, NW), n), (lax.rem(w + 1, NW), n)

    def halo(lv, b, side):
        return pltpu.make_async_remote_copy(
            src_ref=hs.at[lv, b, side], dst_ref=hr.at[lv, b, side], send_sem=hss.at[lv, b, side],
            recv_sem=hrs.at[lv, b, side], device_id=down_dev if side == 0 else up_dev, device_id_type=MESH)

    def extract(lv, b, buf, both):
        base = buf * VSZ + b * (PB * Q * VR_)
        for q in range(Q):
            for at, cnt in groups(PB):
                off = base + (at * Q + q) * VR_
                if both:
                    hs[lv, b, 0, pl.ds(q * PB + at, cnt), :] = vc[pl.ds(off + 23, cnt, stride=Q * VR_), :]
                hs[lv, b, 1, pl.ds(q * PB + at, cnt), :] = vc[pl.ds(off + 8, cnt, stride=Q * VR_), :]

    def send_halo(lv, b):
        @pl.when(w < NW - 1)
        def _():
            halo(lv, b, 0).start()

        @pl.when(w > 0)
        def _():
            halo(lv, b, 1).start()

    def shift_own(b, buf):
        def body(p, _):
            src = pl.multiple_of(buf * VSZ + (b * PB + p) * (Q * VR_), 8)
            dst = pl.multiple_of((b * PB + p) * (Q * VR_), 8)
            for g in range(2):
                tiles = [vc[pl.ds(src + q * VR_ + 8 + 8 * g, 8), :] for q in range(Q)]
                for q, t in enumerate(from_left(tiles)):
                    vl[pl.ds(dst + q * VR_ + 8 + 8 * g, 8), :] = t
                for q, t in enumerate(from_right(tiles)):
                    vr[pl.ds(dst + q * VR_ + 8 + 8 * g, 8), :] = t
            return 0

        lax.fori_loop(0, PB, body, 0, unroll=12)

    def unpack_halo(lv, b, buf):
        for side, row in ((0, 7), (1, 24)):
            for at, cnt in groups(PB):
                tiles = [hr[lv, b, side, pl.ds(q * PB + at, cnt), :] for q in range(Q)]
                base = (b * PB + at) * (Q * VR_)
                for ref, off, vals in ((vc, buf * VSZ, tiles), (vl, 0, from_left(tiles)), (vr, 0, from_right(tiles))):
                    for q in range(Q):
                        ref[pl.ds(off + base + q * VR_ + row, cnt, stride=Q * VR_), :] = vals[q]

    for c in xl:
        c.wait()
    for b in range(NB):
        extract(0, b, 0, True)
    for b in range(NB):
        shift_own(b, 0)

    for c in fl:
        c.wait()
    for q in range(Q):
        for f in range(1, 4):
            for at, cnt in groups(36):
                cs[q, pl.ds((f - 1) * 36 + at, cnt), :] = fv[pl.ds(((f * 36 + at) * Q + q) * FR_ + 23, cnt, stride=Q * FR_), :]
    for at3, (f, step) in enumerate(SHIFTED):
        def body(p, _, at3=at3, f=f, step=step):
            src = pl.multiple_of((f * 36 + p) * (Q * FR_), 8)
            dst = pl.multiple_of((at3 * 36 + p) * (Q * FR_), 8)
            for g in range(2):
                tiles = [fv[pl.ds(src + q * FR_ + 8 + 8 * g, 8), :] for q in range(Q)]
                moved = from_left(tiles) if step == 1 else from_right(tiles)
                for q in range(Q):
                    sh[pl.ds(dst + q * FR_ + 8 + 8 * g, 8), :] = moved[q]
            return 0

        lax.fori_loop(0, 36, body, 0, unroll=12)

    for c in cl + scalars:
        c.wait()

    middle = 0.5 * (cut[0] + top[0])
    half_width = 0.5 * (top[0] - cut[0])

    stencil = [(cv, 16, 0, 0, False, 0, 0)]
    for f, (dr, dc) in enumerate(OFFSETS):
        stencil.append((fv, FR_, f * 36, 8, False, dc, dr))
    for ref, slot, (dr, dc) in ((sh, 0, (0, 1)), (sh, 1, (1, -1)), (fv, 2, (1, 0)), (sh, 2, (1, 1))):
        stencil.append((ref, FR_, slot * 36, 8 - dr, True, -dc, -dr))

    def main_copy(b, dst, sender):
        return pltpu.make_async_remote_copy(
            src_ref=vc4.at[pl.ds(PL + b * PB, PB), dst // 2, pl.ds(pl.multiple_of(8 + 8 * lax.rem(dst, 2), 8), 8)],
            dst_ref=mc4.at[sender, pl.ds(b * PB, PB), pl.ds(0, 8)],
            send_sem=mss.at[b, dst], recv_sem=mrs.at[b, sender], device_id=(w, dst), device_id_type=MESH)

    def own_main(b):
        return pltpu.make_async_copy(
            vc4.at[pl.ds(PL + b * PB, PB), qme, pl.ds(pl.multiple_of(8 + 8 * gme, 8), 8)],
            mc4.at[n, pl.ds(b * PB, PB), pl.ds(0, 8)], locs.at[b])

    def apply(lv, b):
        cur = 0 if isinstance(lv, int) else lax.rem(lv, 2) * VSZ
        nxt = VSZ - cur
        scale = (1.0 if isinstance(lv, int) else 2.0) / half_width
        vb = b * (PB * Q * VR_)

        def body(k, _):
            q = lax.rem(qme + 1 + k, Q)
            vq = q * VR_
            for g in range(2):
                acc = [[None] * J for _ in range(MB)]
                for ref, slot_rows, plane0, row0, transposed, dc, dr in stencil:
                    for j in range(J):
                        src = {0: vc, 1: vr, -1: vl}[dc]
                        base = pl.multiple_of(vb + vq + (cur if dc == 0 else 0), 8)
                        vs = [src[pl.ds(base + (m * J + j) * (Q * VR_) + 8 + 8 * g + dr, 8), :] for m in range(MB)]
                        for i in range(J):
                            plane = plane0 + (j * J + i if transposed else i * J + j)
                            cbase = pl.multiple_of(q * slot_rows, 8)
                            cf = ref[pl.ds(cbase + plane * (Q * slot_rows) + row0 + 8 * g, 8), :]
                            for m in range(MB):
                                term = cf * vs[m]
                                acc[m][i] = term if acc[m][i] is None else acc[m][i] + term
                for m in range(MB):
                    for i in range(J):
                        off = vb + vq
                        at = (m * J + i) * (Q * VR_) + 8 + 8 * g
                        here = vc[pl.ds(pl.multiple_of(off + cur, 8) + at, 8), :]
                        there = pl.ds(pl.multiple_of(off + nxt, 8) + at, 8)
                        vc[there, :] = (acc[m][i] - middle * here) * scale - vc[there, :]

            if not isinstance(lv, int):
                @pl.when((lv == 2) & (k < Q - 1))
                def _():
                    for g in range(2):
                        main_copy(b, 2 * q + g, n).start()

            return 0

        lax.fori_loop(0, Q, body, 0)

    def edge_copy(b, dst, sender):
        return pltpu.make_async_remote_copy(
            src_ref=eps.at[b, dst], dst_ref=epr.at[b, sender], send_sem=ess.at[b, dst], recv_sem=ers.at[b, sender],
            device_id=(w, dst), device_id_type=MESH)

    def own_edge(b):
        return pltpu.make_async_copy(eps.at[b, n], epr.at[b, n], locs.at[NB + b])

    lane = lanes()

    def edges(b):
        @pl.when(w < NW - 1)
        def _():
            halo(3, b, 1).wait_recv()

        def body(q, _):
            right, left = lax.rem(q + 1, Q), lax.rem(q + 3, Q)
            base = VSZ + b * (PB * Q * VR_)
            for g in range(2):
                dst = q * 2 + g
                pack = zero
                for p in range(PB):
                    at = p * (Q * VR_) + 8 + 8 * g
                    vright = vc[pl.ds(pl.multiple_of(base + right * VR_, 8) + at, 8), :]
                    vleft = vc[pl.ds(pl.multiple_of(base + left * VR_, 8) + at, 8), :]
                    pack = jnp.where(lane == 2 * p, vright if p == 0 else pltpu.roll(vright, 2 * p, 1), pack)
                    pack = jnp.where(lane == 2 * p + 1, pltpu.roll(vleft, 2 * p + 2, 1), pack)
                for k, (first, cnt) in enumerate(groups(PB)):
                    def row(at_q):
                        if g == 0:
                            off = pl.multiple_of(base + at_q * VR_, 8) + first * (Q * VR_) + 16
                            return vc[pl.ds(off, cnt, stride=Q * VR_), :]
                        return hr[3, b, 1, pl.ds(at_q * PB + first, cnt), :]

                    eps[b, dst, pl.ds(first, cnt), :] = row(q)
                    pack = jnp.where(lane == 64 + 2 * k, pltpu.roll(whole(row(right)), 64 + 2 * k, 1), pack)
                    pack = jnp.where(lane == 65 + 2 * k, pltpu.roll(whole(row(left)), 66 + 2 * k, 1), pack)
                eps[b, dst, pl.ds(ER, 8), :] = pack
            return 0

        lax.fori_loop(0, Q, body, 0)
        for d in (4, 3, 5, 2, 6, 7, 1):
            edge_copy(b, lax.rem(n + d, NN), n).start()
        own_edge(b).start()

    def step(t, _):
        lv, b = 1 + lax.rem(t, 2), t // 2
        buf = lax.rem(lv, 2)


        @pl.when(w > 0)
        def _():
            halo(lv, b, 0).wait_recv()

        @pl.when(w < NW - 1)
        def _():
            halo(lv, b, 1).wait_recv()

        unpack_halo(lv, b, buf)
        apply(lv, b)
        extract(lv + 1, b, 1 - buf, True)

        @pl.when(lv == 1)
        def _():
            send_halo(lv + 1, b)
            shift_own(b, 1 - buf)

        @pl.when(lv == 2)
        def _():
            @pl.when(w > 0)
            def _():
                halo(3, b, 1).start()

            main_copy(b, 2 * qme + 1 - gme, n).start()
            own_main(b).start()

        return 0

    apply(0, 0)

    pl.semaphore_wait(barrier, NN + NW - 2)
    for b in range(NB):
        send_halo(0, b)

    coef_halo = pltpu.make_async_remote_copy(
        src_ref=cs, dst_ref=ch, send_sem=css, recv_sem=crs, device_id=down_dev, device_id_type=MESH)

    @pl.when(w < NW - 1)
    def _():
        coef_halo.start()

    apply(0, 1)

    for b in range(NB):
        @pl.when(w > 0)
        def _():
            halo(0, b, 0).wait_recv()

        @pl.when(w < NW - 1)
        def _():
            halo(0, b, 1).wait_recv()

    @pl.when(w > 0)
    def _():
        coef_halo.wait_recv()

    def outside(side, j):
        return [jnp.concatenate(
            [hr[0, b, side, pl.ds(q * PB + j, MB, stride=J), :] for b in range(NB)], axis=0) for q in range(Q)]

    def add_row(i, q, row, extra):
        there = pl.ds(VSZ + (i * Q + q) * VR_ + row, ML, stride=J * Q * VR_)
        vc[there, :] = vc[there, :] + extra * (1.0 / half_width)

    above = [outside(0, j) for j in range(J)]
    for i in range(J):
        parts = []
        for f in range(3):
            parts.append([sum(ch[q, pl.ds(f * 36 + j * J + i, 1), :] * above[j][q] for j in range(J)) for q in range(Q)])
        left, right = from_right(parts[0]), from_left(parts[2])
        for q in range(Q):
            add_row(i, q, 8, left[q] + parts[1][q] + right[q])
    below = [outside(1, j) for j in range(J)]
    moved = [[from_left(t) for t in below], below, [from_right(t) for t in below]]
    for i in range(J):
        for q in range(Q):
            add_row(i, q, 23, sum(
                cs[q, pl.ds(f * 36 + i * J + j, 1), :] * moved[f][j][q] for f in range(3) for j in range(J)))
    for b in range(NB):
        extract(1, b, 1, True)
        send_halo(1, b)
    for b in range(NB):
        shift_own(b, 1)
    for at, cnt in groups(36):
        for f, ref, slot, move in ((1, sh, 1, from_right), (2, fv, 2, None), (3, sh, 2, from_left)):
            tiles = [ch[q, pl.ds((f - 1) * 36 + at, cnt), :] for q in range(Q)]
            tiles = tiles if move is None else move(tiles)
            for q in range(Q):
                ref[pl.ds(((slot * 36 + at) * Q + q) * FR_ + 7, cnt, stride=Q * FR_), :] = tiles[q]

    lax.fori_loop(0, 2 * NB, step, 0)

    def own_coef(p, _):
        src = pl.multiple_of(p * (Q * 16) + qme * 16 + 8 * gme, 8)
        k5[pl.ds(pl.multiple_of(p * 8, 8), 8), :] = 0.5 * cv[pl.ds(src, 8), :]
        return 0

    def own_forward(p, _):
        src = pl.multiple_of(p * (Q * FR_) + qme * FR_ + 8 + 8 * gme, 8)
        k5[pl.ds(pl.multiple_of(288 + p * 8, 8), 8), :] = fv[pl.ds(src, 8), :]
        return 0

    lax.fori_loop(0, 36, own_coef, 0, unroll=6)
    lax.fori_loop(0, 144, own_forward, 0, unroll=8)

    for b in range(NB):
        edges(b)
    for b in range(NB):
        for d in range(1, NN):
            main_copy(b, n, lax.rem(n + d, NN)).wait_recv()
        own_main(b).wait()

    def split(v):
        hi = v.astype(BF16)
        return hi, (v - hi.astype(F32)).astype(BF16)

    def fill(ref, slot, at):
        for j in range(J):
            for r in range(8):
                col = pl.ds((j * 8 + r) * 128, 128)
                v = jnp.concatenate(
                    [ref[pl.ds((k * PL + j) * slot + r, 8, stride=J * slot), :] for k in range(NN)], axis=0)
                hi, lo = split(v)
                s[pl.ds(at, 64), col] = hi
                s[pl.ds(at + 64, 64), col] = lo

    def products(at):
        total = jnp.zeros((128, 128), F32)
        for k in range(12):
            col = pl.ds(k * 512, 512)
            total = total + lax.dot_general(
                s[pl.ds(0, 128), col], s[pl.ds(at, 128), col], (((1,), (1,)), ((), ())), preferred_element_type=F32)
        both = total[0:64] + total[64:128]
        return (both + pltpu.roll(both, 64, 1)) / UNKNOWNS

    fill(mc, 16, 0)
    a0[...] = products(0)

    def piece1(dst, sender):
        return pltpu.make_async_remote_copy(
            src_ref=a0.at[pl.ds(pl.multiple_of(dst * 8, 8), 8)], dst_ref=a1.at[sender], send_sem=a1s.at[dst],
            recv_sem=a1r.at[sender], device_id=(w, dst), device_id_type=MESH)

    def piece2(dst, sender):
        return pltpu.make_async_remote_copy(
            src_ref=ps, dst_ref=a2.at[sender], send_sem=a2s.at[dst], recv_sem=a2r.at[sender],
            device_id=(dst, n), device_id_type=MESH)

    def piece3(dst, sender):
        return pltpu.make_async_remote_copy(
            src_ref=pt, dst_ref=a3.at[sender], send_sem=a3s.at[dst], recv_sem=a3r.at[sender],
            device_id=(w, dst), device_id_type=MESH)

    def whole1(dst, sender):
        return pltpu.make_async_remote_copy(
            src_ref=z0, dst_ref=z1.at[sender], send_sem=z1s.at[dst], recv_sem=z1r.at[sender],
            device_id=(w, dst), device_id_type=MESH)

    def whole2(dst, sender):
        return pltpu.make_async_remote_copy(
            src_ref=zp, dst_ref=z2.at[sender], send_sem=z2s.at[dst], recv_sem=z2r.at[sender],
            device_id=(dst, n), device_id_type=MESH)

    def exchange(piece, count, me):
        for d in range(1, count):
            piece(lax.rem(me + d, count), me).start()

    def collect(piece, count, me):
        for d in range(1, count):
            piece(me, lax.rem(me + d, count)).wait_recv()

    def added(ref, count):
        terms = [ref[k] for k in range(count)]
        while len(terms) > 1:
            terms = [terms[k] + terms[k + 1] for k in range(0, len(terms), 2)]
        return terms[0]

    def unpack(b, src):
        base = pl.multiple_of((src * PL + b * PB) * 16, 8)
        pack = epr[b, src, pl.ds(ER, 8), :]
        for p in range(PB):
            v = mc[pl.ds(base + p * 16, 8), :]
            sides = pltpu.roll(pack, 127 - 2 * p, 1)
            mr[pl.ds(base + p * 16, 8), :] = jnp.where(lane == 127, sides, pltpu.roll(v, 127, 1))
            ml[pl.ds(base + p * 16, 8), :] = jnp.where(lane == 0, sides, pltpu.roll(v, 1, 1))
        for k, (first, cnt) in enumerate(groups(PB)):
            h = epr[b, src, pl.ds(first, cnt), :]
            there = pl.ds(base + first * 16 + 8, cnt, stride=16)
            mc[there, :] = h
            mask = lanes(cnt)
            sides = pltpu.roll(pack, 63 - 2 * k, 1)[0:cnt]
            mr[there, :] = jnp.where(mask == 127, sides, pltpu.roll(h, 127, 1))
            ml[there, :] = jnp.where(mask == 0, sides, pltpu.roll(h, 1, 1))

    half_stencil = ((mc, 0), (mr, 0), (ml, 1), (mc, 1), (mr, 1))

    def half_apply(b, src):
        base = pl.multiple_of((src * PL + b * PB) * 16, 8)
        wbase = pl.multiple_of((src * PL + b * PB) * 8, 8)
        acc = [[None] * J for _ in range(MB)]
        for f, (ref, dr) in enumerate(half_stencil):
            for j in range(J):
                vs = [ref[pl.ds(base + (m * J + j) * 16 + dr, 8), :] for m in range(MB)]
                for i in range(J):
                    cf = k5[pl.ds((f * 36 + i * J + j) * 8, 8), :]
                    for m in range(MB):
                        term = cf * vs[m]
                        acc[m][i] = term if acc[m][i] is None else acc[m][i] + term
        for m in range(MB):
            for i in range(J):
                wm[pl.ds(wbase + (m * J + i) * 8, 8), :] = acc[m][i]

    def meet(t, _):
        b, d = t // NN, lax.rem(t, NN)
        src = lax.rem(n + d, NN)

        @pl.when(d == 0)
        def _():
            own_edge(b).wait()

        @pl.when(d > 0)
        def _():
            edge_copy(b, n, src).wait_recv()

        unpack(b, src)
        half_apply(b, src)
        return 0

    def meet_half(half):
        count = NB * NN // 2
        lax.fori_loop(half * count, (half + 1) * count, meet, 0)

    exchange(piece1, NN, n)
    a1[n] = a0[pl.ds(pl.multiple_of(n * 8, 8), 8), :]
    meet_half(0)
    collect(piece1, NN, n)
    ps[...] = added(a1, NN)
    exchange(piece2, NW, w)
    a2[w] = ps[...]
    meet_half(1)
    collect(piece2, NW, w)
    pt[...] = added(a2, NW)
    exchange(piece3, NN, n)
    a3[n] = pt[...]
    fill(wm, 8, 128)
    other = products(128)
    z0[...] = jnp.where(lanes(32) < 64, other[0:32], other[32:64])
    collect(piece3, NN, n)
    gram = jnp.concatenate([a3[k] for k in range(NN)], axis=0)
    exchange(whole1, NN, n)
    z1[n] = z0[...]

    lane64 = lanes(64)
    row64 = lax.broadcasted_iota(jnp.int32, (64, 128), 0)
    work = jnp.where(lane64 < 64, gram, (lane64 - 64 == row64).astype(F32))
    finished = []
    for k0 in range(0, 64, 4):
        first = 8 * len(finished)
        rows = row64[first:]
        column = [jnp.broadcast_to(work[:, k0 + t:k0 + t + 1], work.shape) for t in range(4)]
        line = [work[k0 + t - first:k0 + t - first + 1, :] for t in range(4)]
        for t in range(4):
            at = k0 + t - first
            factor = jnp.where(rows > k0 + t, column[t] * (1.0 / column[t][at:at + 1, :]), 0.0)
            for u in range(t + 1, 4):
                column[u] = column[u] - factor * column[u][at:at + 1, :]
                line[u] = line[u] - factor[at + u - t:at + u - t + 1, :] * line[t]
            work = work - factor * line[t]
        if k0 % 8 == 4:
            finished.append(work[0:8])
            work = work[8:]
    work = jnp.concatenate(finished, axis=0)
    diag = jnp.sum(jnp.where(lane64 == row64, work, 0.0), axis=1, keepdims=True)
    work = work * lax.rsqrt(diag)
    turned = pltpu.roll(work, 64, 1)
    twice = jnp.where(lane64 < 64, turned, work)
    mhi, mlo = split(twice)
    mix = jnp.concatenate([mhi, mlo], axis=0)

    collect(whole1, NN, n)
    zp[...] = added(z1, NN)
    exchange(whole2, NW, w)
    z2[w] = zp[...]

    def back(h, dst):
        return pltpu.make_async_remote_copy(
            src_ref=rb5.at[dst, :, pl.ds(2 * h, 2)],
            dst_ref=out.at[:, pl.ds(2 * h, 2), pl.ds(pl.multiple_of(8 * gme, 8), 8), pl.ds(pl.multiple_of(128 * qme, 128), 128)],
            send_sem=bss.at[h, dst], recv_sem=brs.at[h, n], device_id=(w, dst), device_id_type=MESH)

    def back_arrival(h, sender):
        return pltpu.make_async_remote_copy(
            src_ref=rb5.at[sender, :, pl.ds(2 * h, 2)],
            dst_ref=out.at[:, pl.ds(2 * h, 2), pl.ds(pl.multiple_of(8 * lax.rem(sender, 2), 8), 8),
                           pl.ds(pl.multiple_of(128 * (sender // 2), 128), 128)],
            send_sem=bss.at[h, sender], recv_sem=brs.at[h, sender], device_id=(w, sender), device_id_type=MESH)

    def own_back(h):
        return pltpu.make_async_copy(
            rb5.at[n, :, pl.ds(2 * h, 2)],
            out.at[:, pl.ds(2 * h, 2), pl.ds(pl.multiple_of(8 * gme, 8), 8), pl.ds(pl.multiple_of(128 * qme, 128), 128)],
            locs.at[2 * NB + h])

    for tile in range(24):
        col = pl.ds(tile * 256, 256)
        both = jnp.dot(mix, s[pl.ds(0, 128), col], preferred_element_type=F32)
        basis = both[0:64] + both[64:128]
        for half in range(2):
            j, r = divmod(tile * 2 + half, 8)
            for k in range(NN):
                rb[pl.ds((k * PL + j) * 8 + r, 8, stride=J * 8), :] = basis[8 * k:8 * k + 8, 128 * half:128 * half + 128]
        if tile % 8 == 7:
            for d in (4, 3, 5, 2, 6, 7, 1):
                back(tile // 8, lax.rem(n + d, NN)).start()
            own_back(tile // 8).start()


    collect(whole2, NW, w)
    other = added(z2, NW)
    other = jnp.concatenate([other, pltpu.roll(other, 64, 1)], axis=0)

    minv = jnp.where(lane64 < 64, turned, 0.0)[:, 0:64]
    zmat = other[:, 0:64]
    half = jnp.dot(minv, zmat, precision=HIGHEST, preferred_element_type=F32) + lax.dot_general(
        minv, zmat, (((1,), (1,)), ((), ())), precision=HIGHEST, preferred_element_type=F32)
    pv[...] = lax.dot_general(half, minv, (((1,), (1,)), ((), ())), precision=HIGHEST, preferred_element_type=F32)

    projected = pltpu.make_async_copy(pv, proj, locs.at[2 * NB + 3])
    projected.start()
    projected.wait()

    for lv in range(3):
        for b in range(NB):
            @pl.when(w < NW - 1)
            def _():
                halo(lv, b, 0).wait_send()
    for lv in range(4):
        for b in range(NB):
            @pl.when(w > 0)
            def _():
                halo(lv, b, 1).wait_send()

    @pl.when(w < NW - 1)
    def _():
        coef_halo.wait_send()

    for d in range(1, NN):
        dst = lax.rem(n + d, NN)
        for b in range(NB):
            main_copy(b, dst, n).wait_send()
            edge_copy(b, dst, n).wait_send()
        piece1(dst, n).wait_send()
        piece3(dst, n).wait_send()
        whole1(dst, n).wait_send()
    for d in range(1, NW):
        piece2(lax.rem(w + d, NW), w).wait_send()
        whole2(lax.rem(w + d, NW), w).wait_send()
    for h in range(3):
        own_back(h).wait()
        for d in range(1, NN):
            back(h, lax.rem(n + d, NN)).wait_send()
            back_arrival(h, lax.rem(n + d, NN)).wait_recv()


def hand_over(basis, projected, basis_out, projected_out, held, small, sems):
    pairs = [(basis.at[m], held.at[m], basis_out.at[m]) for m in range(ML)] + [(projected, small, projected_out)]
    arriving = [pltpu.make_async_copy(src, mid, sems.at[0, k]) for k, (src, mid, _) in enumerate(pairs)]
    leaving = [pltpu.make_async_copy(mid, dst, sems.at[1, k]) for k, (_, mid, dst) in enumerate(pairs)]
    for c in arriving:
        c.start()
    for c, d in zip(arriving, leaving):
        c.wait()
        d.start()
    for d in leaving:
        d.wait()


def local(start_block, center_block, forward_blocks, filter_cut, filter_top):
    dma = pltpu.SemaphoreType.DMA
    vm = lambda *shape: pltpu.VMEM(shape, F32)
    anyspace = pl.BlockSpec(memory_space=pl.ANY)
    basis, projected = pl.pallas_call(
        kernel,
        out_shape=(jax.ShapeDtypeStruct((ML, J, 16, 512), F32), jax.ShapeDtypeStruct((64, 64), F32)),
        in_specs=[anyspace] * 5,
        out_specs=(anyspace, anyspace),
        scratch_shapes=[
            pltpu.SMEM((1,), F32), pltpu.SMEM((1,), F32),
            vm(2 * VSZ, 128), vm(VSZ, 128), vm(VSZ, 128),
            vm(36 * Q * 16, 128), vm(144 * Q * FR_, 128), vm(108 * Q * FR_, 128),
            vm(Q, 112, 128), vm(Q, 112, 128),
            vm(4, NB, 2, Q * PB, 128), vm(4, NB, 2, Q * PB, 128),
            vm(NB, NN, ER + 8, 128), vm(NB, NN, ER + 8, 128),
            vm(NN * PL * 16, 128), vm(NN * PL * 16, 128), vm(NN * PL * 16, 128),
            vm(180 * 8, 128), vm(NN * PL * 8, 128), pltpu.VMEM((256, 6144), BF16), vm(NN * PL * 8, 128),
            vm(64, 128), vm(NN, 8, 128), vm(8, 128), vm(NW, 8, 128), vm(8, 128), vm(NN, 8, 128), vm(64, 64),
            vm(32, 128), vm(NN, 32, 128), vm(32, 128), vm(NW, 32, 128),
            dma((14,)), dma((4, NB, 2)), dma((4, NB, 2)), dma(()), dma(()),
            dma((NB, NN)), dma((NB, NN)), dma((NB, NN)), dma((NB, NN)),
            dma((NN,)), dma((NN,)), dma((NW,)), dma((NW,)), dma((NN,)), dma((NN,)),
            dma((NN,)), dma((NN,)), dma((NW,)), dma((NW,)), dma((3, NN)), dma((3, NN)),
            dma((2 * NB + 4,)),
        ],
        compiler_params=pltpu.CompilerParams(
            collective_id=0, has_side_effects=True, vmem_limit_bytes=60 * 1024 * 1024),
    )(start_block, center_block, forward_blocks, filter_cut, filter_top)
    return pl.pallas_call(
        hand_over,
        out_shape=(jax.ShapeDtypeStruct(basis.shape, F32), jax.ShapeDtypeStruct(projected.shape, F32)),
        in_specs=[anyspace] * 2,
        out_specs=(anyspace, anyspace),
        scratch_shapes=[vm(ML, J, 16, 512), vm(64, 64), dma((2, ML + 1))],
    )(basis, projected)


def solution(mesh):
    in_specs = (
        P("narrow", None, "wide", None),
        P(None, None, "wide", None),
        P(None, None, None, "wide", None),
        P(),
        P(),
    )
    out_specs = (P("narrow", None, "wide", None), P())
    return jax.shard_map(local, mesh=mesh, in_specs=in_specs, out_specs=out_specs, check_vma=False)
```
